32 devices in a mesh: gx: 8 (over z, core), gy: 4 (over y, x).
Axes of the slice: x: 2, y: 2, z: 4, core: 2. Of those that a mesh axis runs over, the one named last changes fastest.
Arguments:
- patches: bfloat16 [8, 64, 128, 512], P(None, None, 'gx', 'gy'), may hold values from -6 to 6
- patch_wx: bfloat16 [8, 4, 128], P(None, 'gy', 'gx'), may hold values from 1 to 3
- patch_wy: bfloat16 [8, 8, 512], P(None, 'gx', 'gy'), may hold values from 1 to 3
- offset_x: int32 [8, 8, 4], P(None, 'gx', 'gy'), may hold values from 0 to 15
- offset_y: int32 [8, 8, 4], P(None, 'gx', 'gy'), may hold values from 0 to 127
- block_counts: int32 [8, 4], P('gx', 'gy'), may hold values from 2 to 8, as said below
- template: bfloat16 [64, 128, 512], P(None, 'gx', 'gy'), may hold values from -6 to 6
- stiff_mu: float32 [64, 128, 512], P(None, 'gx', 'gy'), may hold values from 0.5 to 2
- stiff_lam: float32 [64, 128, 512], P(None, 'gx', 'gy'), may hold values from 0.5 to 4
- start_field: float32 [3, 64, 128, 512], P(None, None, 'gx', 'gy'), may hold values from -4 to 4
Outputs:
- joined: bfloat16 [64, 128, 512], P(None, 'gx', 'gy')
- field: float32 [3, 64, 128, 512], P(None, None, 'gx', 'gy')
The draws below stay inside these ranges and needn't reach their ends.
Inputs may be any that keep to these rules, and one draw needn't show every extreme that they name: `block_counts`: a block's patch slots at or beyond its count are unused; some block holds exactly 8 live patches.
All inputs are finite; a program needn't handle non-finite values.
Results may differ from the reference program's by a relative error of at most 0.0045.
Values may be sent and summed in bfloat16 or wider, within the bound.
A program may use at most 128 MiB of HBM per device.

```python
import math
import jax
import jax.numpy as jnp
from jax import lax

BX = 16
BY = 128
Z = 64
SLOTS = 8
PASSES = 4
NX = 128
NY = 512
N_GX = 8
N_GY = 4


def draw_block_counts(key, part):
    key_base, key_heavy, key_pick = jax.random.split(key, 3)
    base_count = jax.random.randint(key_base, (N_GX, N_GY), 2, SLOTS // 2 + 2)
    heavy = jax.random.randint(key_heavy, (N_GX, N_GY), 0, 8) == 0
    chosen = jax.random.randint(key_pick, (), 0, N_GX * N_GY)
    position = jnp.arange(N_GX * N_GY).reshape(N_GX, N_GY)
    filled = heavy | (position == chosen)
    return jnp.where(filled, SLOTS, jnp.minimum(base_count, SLOTS)).astype(jnp.int32)


def touch_ends(entries, own_key, low, top_value):
    longest = entries.shape.index(max(entries.shape))
    spots = []
    for shift in (0, 1):
        where = [jax.random.randint(jax.random.fold_in(own_key, axis), (), 0, length) for axis, length in enumerate(entries.shape)]
        where[longest] = (where[longest] + shift) % entries.shape[longest]
        spots.append(tuple(where))
    return entries.at[spots[0]].set(low).at[spots[1]].set(top_value)


def block_scale(key, extent, pieces, low, largest):
    level, own = 1.0, jax.random.fold_in(key, 6)
    for dim, blocks in pieces:
        heights = jnp.exp(jax.random.uniform(jax.random.fold_in(own, dim), (blocks,), jnp.float32, low / len(pieces), largest / len(pieces)))
        level = level * jnp.repeat(heights, extent[dim] // blocks).reshape([-1 if axis == dim else 1 for axis in range(len(extent))])
    return level


def gaussian(rng, dims, width, limit, shards=(), held_as=jnp.bfloat16):
    array = width * jax.random.normal(rng, dims, jnp.float32)
    if shards:
        array = array * block_scale(rng, dims, shards, -0.22, 0.18)
    return jnp.clip(array, -limit, limit).astype(held_as)


def setup_inputs(seed: int = 0) -> dict:
    streams_of = jax.random.split(jax.random.key(seed), 11)
    patches = gaussian(streams_of[0], (SLOTS, Z, NX, NY), 1.0, 6.0, ((2, 8), (3, 4)))
    patch_wx = jnp.clip(jnp.exp(math.log(3.0) - 1.0986123 * jax.random.uniform(streams_of[1], (SLOTS, N_GY, NX), jnp.float32) ** block_scale(streams_of[1], (SLOTS, N_GY, NX), ((1, 4), (2, 8)), -0.2, 0.2)), 1.0, 3.0).astype(jnp.bfloat16)
    patch_wy = jnp.clip(jnp.exp(math.log(3.0) - 1.0986123 * jax.random.uniform(streams_of[2], (SLOTS, N_GX, NY), jnp.float32) ** block_scale(streams_of[2], (SLOTS, N_GX, NY), ((1, 8), (2, 4)), -0.2, 0.2)), 1.0, 3.0).astype(jnp.bfloat16)
    offset_x = touch_ends(jax.random.randint(streams_of[3], (SLOTS, N_GX, N_GY), 0, BX), jax.random.fold_in(streams_of[3], 1), 0, BX - 1).astype(jnp.int32)
    offset_y = touch_ends(jax.random.randint(streams_of[4], (SLOTS, N_GX, N_GY), 0, BY), jax.random.fold_in(streams_of[4], 1), 0, BY - 1).astype(jnp.int32)
    block_counts = draw_block_counts(jax.random.fold_in(streams_of[10], 71), 0)
    template = gaussian(streams_of[6], (Z, NX, NY), 1.0, 6.0, ((1, 8), (2, 4)))
    stiff_mu = jnp.clip(jnp.exp(math.log(2.0) - 1.3862944 * jax.random.uniform(streams_of[7], (Z, NX, NY), jnp.float32) ** block_scale(streams_of[7], (Z, NX, NY), ((1, 8), (2, 4)), -0.2, 0.2)), 0.5, 2.0)
    stiff_lam = jnp.clip(jnp.exp(math.log(4.0) - 2.0794415 * jax.random.uniform(streams_of[8], (Z, NX, NY), jnp.float32) ** block_scale(streams_of[8], (Z, NX, NY), ((1, 8), (2, 4)), -0.2, 0.2)), 0.5, 4.0)
    start_field = gaussian(streams_of[9], (3, Z, NX, NY), 0.5, 4.0, ((2, 8), (3, 4)), jnp.float32)
    return dict(patches=patches, patch_wx=patch_wx, patch_wy=patch_wy, offset_x=offset_x, offset_y=offset_y, block_counts=block_counts, template=template, stiff_mu=stiff_mu, stiff_lam=stiff_lam, start_field=start_field)


RELAX_FACTOR = 0.9
STEPS_UNIT = ((1, 0, 0), (0, 1, 0), (0, 0, 1))


def window(array_in, move_z, move_x, move_y):
    size_z = array_in.shape[-3] - 4
    size_x = array_in.shape[-2] - 4
    size_y = array_in.shape[-1] - 4
    return array_in[..., 2 + move_z:2 + move_z + size_z, 2 + move_x:2 + move_x + size_x, 2 + move_y:2 + move_y + size_y]


def moved(base, step_dir, factor):
    return (base[0] + factor * step_dir[0], base[1] + factor * step_dir[1], base[2] + factor * step_dir[2])


def divergence(padded, at_pos):
    result = 0.0
    for dim_idx in range(3):
        ahead = moved(at_pos, STEPS_UNIT[dim_idx], 1)
        behind = moved(at_pos, STEPS_UNIT[dim_idx], -1)
        result = result + 0.5 * (window(padded[dim_idx], *ahead) - window(padded[dim_idx], *behind))
    return result


def relax_pass(padded, shear, bulk, rate, forcing):
    shear_here = window(shear, 0, 0, 0)
    updated = []
    for comp_idx in range(3):
        values = padded[comp_idx]
        centre = window(values, 0, 0, 0)
        laplace = 0.0
        for dim_idx in range(3):
            ahead = STEPS_UNIT[dim_idx]
            behind = moved((0, 0, 0), ahead, -1)
            laplace = laplace + 0.5 * (shear_here + window(shear, *ahead)) * (window(values, *ahead) - centre)
            laplace = laplace - 0.5 * (shear_here + window(shear, *behind)) * (centre - window(values, *behind))
        ahead = STEPS_UNIT[comp_idx]
        behind = moved((0, 0, 0), ahead, -1)
        grad_div = 0.5 * (window(bulk, *ahead) * divergence(padded, ahead) - window(bulk, *behind) * divergence(padded, behind))
        updated.append(centre + rate * (laplace + grad_div + forcing[comp_idx]))
    return jnp.stack(updated)


def force_field(images):
    joined_ext = images[0].astype(jnp.float32)
    template_ext = images[1].astype(jnp.float32)
    centre = joined_ext[:, 1:-1, 1:-1]
    mismatch = template_ext[:, 1:-1, 1:-1] - centre
    padded_z = jnp.pad(centre, ((1, 1), (0, 0), (0, 0)))
    slope_z = 0.5 * (padded_z[2:] - padded_z[:-2])
    slope_x = 0.5 * (joined_ext[:, 2:, 1:-1] - joined_ext[:, :-2, 1:-1])
    slope_y = 0.5 * (joined_ext[:, 1:-1, 2:] - joined_ext[:, 1:-1, :-2])
    return jnp.stack([slope_z * mismatch, slope_x * mismatch, slope_y * mismatch])


def reference(patches, patch_wx, patch_wy, offset_x, offset_y, block_counts, template, stiff_mu, stiff_lam, start_field):
    def add_patch(flat, carry):
        weighted, weight_sum = carry
        flat = flat.astype(jnp.int32)
        col_i = flat // (N_GY * SLOTS)
        row_j = (flat // SLOTS) % N_GY
        slot_idx = flat % SLOTS
        start_x = (col_i * BX + offset_x[slot_idx, col_i, row_j]).astype(jnp.int32)
        start_y = (row_j * BY + offset_y[slot_idx, col_i, row_j]).astype(jnp.int32)
        zero_idx = jnp.zeros((), jnp.int32)
        piece = lax.dynamic_slice(patches, (slot_idx, zero_idx, (col_i * BX).astype(jnp.int32), (row_j * BY).astype(jnp.int32)), (1, Z, BX, BY))[0]
        along_x = lax.dynamic_slice(patch_wx, (slot_idx, row_j, (col_i * BX).astype(jnp.int32)), (1, 1, BX))[0, 0].astype(jnp.float32)
        along_y = lax.dynamic_slice(patch_wy, (slot_idx, col_i, (row_j * BY).astype(jnp.int32)), (1, 1, BY))[0, 0].astype(jnp.float32)
        live = (slot_idx < block_counts[col_i, row_j]).astype(jnp.float32)
        weights = along_x[:, None] * along_y[None, :] * live
        region = lax.dynamic_slice(weighted, (zero_idx, start_x, start_y), (Z, BX, BY))
        weighted = lax.dynamic_update_slice(weighted, region + piece.astype(jnp.float32) * weights[None], (zero_idx, start_x, start_y))
        plane = lax.dynamic_slice(weight_sum, (start_x, start_y), (BX, BY))
        weight_sum = lax.dynamic_update_slice(weight_sum, plane + weights, (start_x, start_y))
        return weighted, weight_sum

    initial = (jnp.zeros((Z, NX + BX, NY + BY), jnp.float32), jnp.zeros((NX + BX, NY + BY), jnp.float32))
    weighted, weight_sum = lax.fori_loop(0, N_GX * N_GY * SLOTS, add_patch, initial)
    joined = (weighted[:, :NX, :NY] / jnp.maximum(weight_sum[:NX, :NY], 1.0)[None]).astype(jnp.bfloat16)
    bulk = stiff_lam + stiff_mu
    rate = RELAX_FACTOR / (6.0 * stiff_mu + 3.0 * bulk)
    images = jnp.pad(jnp.stack([joined, template]), ((0, 0), (0, 0), (1, 1), (1, 1)))
    forcing = force_field(images)
    shear_pad = jnp.pad(stiff_mu, 2)
    bulk_pad = jnp.pad(bulk, 2)
    field = start_field
    for pass_idx in range(PASSES):
        widened = jnp.pad(field, ((0, 0), (2, 2), (2, 2), (2, 2)))
        field = relax_pass(widened, shear_pad, bulk_pad, rate, forcing)
    return joined, field
```

```python
import functools

import jax
import jax.numpy as jnp
from jax import lax
from jax.experimental import pallas as pl
from jax.experimental.pallas import tpu as pltpu
from jax.sharding import PartitionSpec as P

PASSES = 4
RELAX_FACTOR = 0.9
F32 = jnp.float32
BF16 = jnp.bfloat16
MESH = pl.DeviceIdType.MESH
DIRS = ((1, 0), (-1, 0), (0, 1), (0, -1), (1, 1), (1, -1), (-1, 1), (-1, -1))
CHUNKS = 4
GROUP = 8


def blend_kernel(count, ox_ref, oy_ref, wx_ref, patches, wy_ref, q00, qx, q01, wout, canvas, wcan, res):
    rows, by = patches.shape[1:]
    bx, depth = q00.shape[:2]
    canvas[...] = jnp.zeros_like(canvas)
    wcan[...] = jnp.zeros_like(wcan)
    source = lax.broadcasted_iota(jnp.int32, (by, 2 * by), 0)
    target = lax.broadcasted_iota(jnp.int32, (by, 2 * by), 1)

    def add_patch(s, carry):
        ox = ox_ref[s, 0]
        place = jnp.where(target == source + oy_ref[s, 0], 1.0, 0.0).astype(BF16)
        moved = jnp.dot(patches[s], place, preferred_element_type=F32)
        res[0] = moved[:, :by]
        res[1] = moved[:, by:]
        along_y = jnp.broadcast_to(wy_ref[s].astype(F32), (16, by)).astype(BF16)
        wy_row = jnp.dot(along_y, place, preferred_element_type=F32)[:8]
        for x in range(bx):
            wx = wx_ref[s, x]
            for h in range(2):
                weight = wx * wy_row[:, h * by : (h + 1) * by]
                canvas[h, ox + x] += res[h, pl.ds(x, depth, stride=bx), :] * weight[0:1]
                wcan[h, ox + x] += weight
        return carry

    lax.fori_loop(0, count[0, 0], add_patch, 0)
    q00[...] = canvas[0, :bx]
    qx[:, 0] = canvas[0, bx:].astype(BF16)
    qx[:, 1] = canvas[1, bx:].astype(BF16)
    q01[...] = canvas[1, :bx].astype(BF16)
    for x in range(bx):
        wout[0, x : x + 1] = wcan[0, x, 0:1]
        wout[1, x : x + 1] = wcan[0, bx + x, 0:1]
        wout[2, x : x + 1] = wcan[1, bx + x, 0:1]
        wout[3, x : x + 1] = wcan[1, x, 0:1]


def relax_kernel(
    q00, qx, q01, wq, tmpl, mu_ref, lam_ref, fld, jout, fout,
    field, mu, qb, coef, force, joined, tall, grad, acc, packed, cpack, wsum,
    land_q, land_w, sy, sw, land_y, land_wy,
    xs, xl, ap, al, dl, cxs, cxl, cap, cal, jxs, jxl, jap, jal,
    send_sem, recv_sem,
):
    bx, depth, by = q00.shape
    gx, gy = lax.axis_index("gx"), lax.axis_index("gy")
    nx, ny = lax.axis_size("gx"), lax.axis_size("gy")

    def exists(d):
        ok = True
        for where, step, count in ((gx, d[0], nx), (gy, d[1], ny)):
            if step == 1:
                ok = jnp.logical_and(ok, where < count - 1)
            if step == -1:
                ok = jnp.logical_and(ok, where > 0)
        return ok

    def opposite(d):
        return (-d[0], -d[1])

    pending = []

    def rdma(src, dst, idx, d):
        return pltpu.make_async_remote_copy(
            src_ref=src, dst_ref=dst, send_sem=send_sem.at[idx], recv_sem=recv_sem.at[idx],
            device_id=(gx + d[0], gy + d[1]), device_id_type=MESH,
        )

    counter = [0]

    def send(src, dst, d):
        idx = counter[0]
        counter[0] += 1

        @pl.when(exists(d))
        def _():
            rdma(src, dst, idx, d).start()

        pending.append((src, dst, idx, d))

        def arrive():
            @pl.when(exists(opposite(d)))
            def _():
                rdma(src, dst, idx, d).wait_recv()

        return arrive

    lane = lax.broadcasted_iota(jnp.int32, (depth, by), 1)
    level = lax.broadcasted_iota(jnp.int32, (depth, by), 0)
    pos = lax.rem(lane, GROUP)

    def strided(x):
        return pl.ds(x, depth, stride=bx)

    def z_next(v):
        return jnp.where(level == depth - 1, 0.0, pltpu.roll(v, depth - 1, 0))

    def z_prev(v):
        return jnp.where(level == 0, 0.0, pltpu.roll(v, 1, 0))

    def y_next(v, edge):
        return jnp.where(lane == by - 1, edge, pltpu.roll(v, by - 1, 1))

    def y_prev(v, edge):
        return jnp.where(lane == 0, edge, pltpu.roll(v, 1, 1))

    def at_edge(pack, x):
        return pltpu.roll(pack, by - 4 - GROUP * x, 1)

    def pack_in(slot, plane, x):
        own = jnp.logical_and(lane >= GROUP * x, lane < GROUP * x + 4)
        acc[slot] = jnp.where(own, pltpu.roll(plane, GROUP * x + 2, 1), acc[slot])

    def merge(own, left, right):
        left, right = left.astype(F32), right.astype(F32)
        out = jnp.where(pos >= 6, pltpu.roll(own, 4, 1), own)
        out = jnp.where(pos == 2, pltpu.roll(left, 2, 1), out)
        out = jnp.where(pos == 4, pltpu.roll(left, 3, 1), out)
        out = jnp.where(pos == 3, pltpu.roll(right, 1, 1), out)
        return jnp.where(pos == 5, pltpu.roll(right, 2, 1), out)

    barrier = pltpu.get_barrier_semaphore()
    total = 0
    for d in DIRS:
        @pl.when(exists(d))
        def _(d=d):
            pl.semaphore_signal(barrier, inc=1, device_id=(gx + d[0], gy + d[1]), device_id_type=MESH)

        total = total + jnp.where(exists(d), 1, 0)
    pl.semaphore_wait(barrier, total)

    step = bx // CHUNKS
    got_q = []
    for c in range(CHUNKS):
        part = pl.ds(c * step, step)
        got_q.append(send(qx.at[part], land_q.at[part], (1, 0)))
    got_w = send(wq.at[pl.ds(1, 2)], land_w, (1, 0))

    for k, d in enumerate(DIRS):
        @pl.when(jnp.logical_not(exists(opposite(d))))
        def _(k=k):
            if k == 0:
                land_q[...] = jnp.zeros_like(land_q)
                land_w[...] = jnp.zeros_like(land_w)
            if k == 2:
                land_y[...] = jnp.zeros_like(land_y)
                land_wy[...] = jnp.zeros_like(land_wy)
            if k < 2:
                for p in range(PASSES):
                    xl[p, k] = jnp.zeros(xl.shape[2:], BF16)
                cxl[k] = jnp.zeros(cxl.shape[1:], BF16)
                jxl[k] = jnp.zeros(jxl.shape[1:], BF16)
            elif k < 4:
                for p in range(PASSES):
                    al[p, k - 2] = jnp.zeros(al.shape[2:], BF16)
                cal[k - 2] = jnp.zeros(cal.shape[1:], BF16)
                jal[k - 2] = jnp.zeros(jal.shape[1:], BF16)
            else:
                for p in range(PASSES):
                    dl[p, k - 4] = jnp.zeros(dl.shape[2:], BF16)

    acc[...] = jnp.zeros_like(acc)

    def load(x, carry):
        for c in range(3):
            plane = fld[c, strided(x), :]
            field[0, c, x + 2] = plane
            pack_in(c, plane, x)
        mu_plane = mu_ref[strided(x), :]
        bulk = lam_ref[strided(x), :] + mu_plane
        mu[x + 1] = mu_plane
        qb[x + 1] = bulk
        pack_in(3, mu_plane, x)
        pack_in(4, bulk, x)
        return carry

    lax.fori_loop(0, bx, load, 0)

    def send_field(p, b):
        for c in range(3):
            xs[p, 0, c] = field[b, c, bx : bx + 2].astype(BF16)
            xs[p, 1, c] = field[b, c, 2:4].astype(BF16)
            ap[p, c] = acc[c].astype(BF16)
        got = [send(xs.at[p, k], xl.at[p, k], DIRS[k]) for k in range(2)]
        got += [send(ap.at[p], al.at[p, k - 2], DIRS[k]) for k in range(2, 4)]
        got += [send(ap.at[p, pl.ds(1, 2)], dl.at[p, k - 4], DIRS[k]) for k in range(4, 8)]
        return got

    got_field = send_field(0, 0)
    for k, at in ((0, bx), (1, 1)):
        cxs[k, 0] = mu[at].astype(BF16)
        cxs[k, 1] = qb[at].astype(BF16)
    cap[...] = acc[3:5].astype(BF16)
    got_coef = [send(cxs.at[k], cxl.at[k], DIRS[k]) for k in range(2)]
    got_coef += [send(cap, cal.at[k - 2], DIRS[k]) for k in range(2, 4)]

    got_w()
    sw[...] = wq[3] + land_w[1]
    got_wy = send(sw, land_wy, (0, 1))
    got_y = []
    for c in range(CHUNKS):
        part = pl.ds(c * step, step)
        got_q[c]()
        sy[part] = (q01[part].astype(F32) + land_q[part, 1].astype(F32)).astype(BF16)
        got_y.append(send(sy.at[part], land_y.at[part], (0, 1)))

    for arrive in got_coef:
        arrive()
    for k, at in ((0, 0), (1, bx + 1)):
        mu[at] = cxl[k, 0].astype(F32)
        qb[at] = cxl[k, 1].astype(F32)
    for c in range(2):
        cpack[c] = merge(acc[3 + c], cal[0, c], cal[1, c])
    cpack[1] = 0.25 * cpack[1]

    def coefficients(x, carry):
        here = mu[x + 1]
        rate = RELAX_FACTOR / (6.0 * here + 3.0 * qb[x + 1])
        half = 0.5 * rate
        edge = at_edge(cpack[0], x)
        near = (
            z_next(here), z_prev(here), mu[x + 2], mu[x], y_next(here, edge), y_prev(here, edge),
        )
        rest = 1.0
        for n, other in enumerate(near):
            one = half * (here + other)
            coef[n, x] = one
            rest = rest - one
        coef[6, x] = rest
        coef[7, x] = rate
        return carry

    lax.fori_loop(0, bx, coefficients, 0)

    def scale(x, carry):
        qb[x] = 0.25 * qb[x]
        return carry

    lax.fori_loop(0, bx + 2, scale, 0)

    def relax(p, got):
        b, nb = p % 2, 1 - p % 2
        last = p == PASSES - 1
        for arrive in got:
            arrive()
        for c in range(3):
            field[b, c, 0:2] = xl[p, 0, c].astype(F32)
            field[b, c, bx + 2 : bx + 4] = xl[p, 1, c].astype(F32)
            packed[c] = merge(acc[c], al[p, 0, c], al[p, 1, c])
        corner = [[dl[p, k, c].astype(F32) for c in range(2)] for k in range(4)]
        top = GROUP * (bx - 1)

        def bring(k, c, at):
            plus_x, plus_y = DIRS[4 + k]
            source = (top if plus_x == 1 else 0) + (1 if plus_y == 1 else 2)
            return pltpu.roll(corner[k][c], (at - source) % by, 1)

        def edge_corners(low, high):
            return jnp.where(lane == 0, bring(low, 1, 0), bring(high, 1, by - 1))

        vx = packed[1]
        ahead = pltpu.roll(vx, by - GROUP, 1)
        ahead = jnp.where(lane == top + 3, bring(3, 0, top + 3), ahead)
        ahead = jnp.where(lane == top + 4, bring(2, 0, top + 4), ahead)
        behind = pltpu.roll(vx, GROUP, 1)
        behind = jnp.where(lane == 3, bring(1, 0, 3), behind)
        behind = jnp.where(lane == 4, bring(0, 0, 4), behind)
        if GROUP * bx < by:
            ahead = jnp.where(lane >= GROUP * bx, 0.0, ahead)
        vz, vy = packed[0], packed[2]
        packed[3] = cpack[1] * (
            (ahead - behind) + (z_next(vz) - z_prev(vz))
            + (pltpu.roll(vy, by - 2, 1) - pltpu.roll(vy, 2, 1))
        )

        def gradient(at, edge):
            vz, vy = field[b, 0, at + 1], field[b, 2, at + 1]
            grad[at] = qb[at] * (
                (field[b, 1, at + 2] - field[b, 1, at])
                + (z_next(vz) - z_prev(vz))
                + (y_next(vy, edge) - y_prev(vy, edge))
            )

        gradient(0, edge_corners(0, 1))
        gradient(bx + 1, edge_corners(2, 3))

        def inner(x, carry):
            gradient(x + 1, at_edge(packed[2], x))
            return carry

        lax.fori_loop(0, bx, inner, 0)
        if not last:
            acc[0:3] = jnp.zeros((3, depth, by), F32)

        def update(x, carry):
            g = grad[x + 1]
            g_edge = at_edge(packed[3], x)
            rise = (
                z_next(g) - z_prev(g),
                grad[x + 2] - grad[x],
                y_next(g, g_edge) - y_prev(g, g_edge),
            )
            k = [coef[n, x] for n in range(8)]
            for c in range(3):
                v = field[b, c, x + 2]
                edge = at_edge(packed[c], x)
                new = k[6] * v + k[7] * rise[c]
                new = new + k[0] * z_next(v) + k[1] * z_prev(v)
                new = new + k[2] * field[b, c, x + 3] + k[3] * field[b, c, x + 1]
                new = new + k[4] * y_next(v, edge) + k[5] * y_prev(v, edge)
                if p > 0:
                    new = new + force[c, x]
                if last:
                    fout[c, strided(x), :] = new
                else:
                    field[nb, c, x + 2] = new
                    if p > 0:
                        pack_in(c, new, x)
            return carry

        lax.fori_loop(0, bx, update, 0)

    relax(0, got_field)

    got_wy()
    wsum[...] = jnp.maximum(wq[0] + land_w[0] + land_wy[...], 1.0)
    acc[3] = jnp.zeros((depth, by), F32)
    tall[...] = tmpl[...].astype(F32)

    def join(x, carry):
        value = q00[x] + land_q[x, 0].astype(F32) + land_y[x].astype(F32)
        plane = (value / wsum[pl.ds(x, 1), :]).astype(BF16).astype(F32)
        joined[x + 1] = plane
        pack_in(3, plane, x)
        return carry

    for c in range(CHUNKS):
        got_y[c]()
        lax.fori_loop(c * step, (c + 1) * step, join, 0)
    jxs[0] = joined[bx].astype(BF16)
    jxs[1] = joined[1].astype(BF16)
    jap[...] = acc[3].astype(BF16)
    got = [send(jxs.at[k], jxl.at[k], DIRS[k]) for k in range(2)]
    got += [send(jap, jal.at[k - 2], DIRS[k]) for k in range(2, 4)]
    for arrive in got:
        arrive()
    joined[0] = jxl[0].astype(F32)
    joined[bx + 1] = jxl[1].astype(F32)
    cpack[0] = merge(acc[3], jal[0], jal[1])

    def forcing(x, carry):
        here = joined[x + 1]
        edge = at_edge(cpack[0], x)
        mismatch = (tall[strided(x), :] - here) * 0.5 * coef[7, x]
        tall[strided(x), :] = here
        slopes = (
            z_next(here) - z_prev(here),
            joined[x + 2] - joined[x],
            y_next(here, edge) - y_prev(here, edge),
        )
        for c in range(3):
            one = mismatch * slopes[c]
            force[c, x] = one
            new = field[1, c, x + 2] + one
            field[1, c, x + 2] = new
            pack_in(c, new, x)
        return carry

    lax.fori_loop(0, bx, forcing, 0)
    got_field = send_field(1, 1)
    jout[...] = tall[...].astype(BF16)
    for p in range(1, PASSES):
        relax(p, got_field)
        if p < PASSES - 1:
            got_field = send_field(p + 1, (p + 1) % 2)
    for src, dst, idx, d in pending:
        @pl.when(exists(d))
        def _(src=src, dst=dst, idx=idx, d=d):
            rdma(src, dst, idx, d).wait_send()


def per_device(
    patches, patch_wx, patch_wy, offset_x, offset_y, block_counts, template, stiff_mu, stiff_lam, start_field
):
    slots, depth, bx, by = patches.shape
    vmem = pl.BlockSpec(memory_space=pltpu.VMEM)
    smem = pl.BlockSpec(memory_space=pltpu.SMEM)
    plane = (depth, by)
    shape = jax.ShapeDtypeStruct
    quads = pl.pallas_call(
        blend_kernel,
        out_shape=(
            shape((bx,) + plane, F32),
            shape((bx, 2) + plane, BF16),
            shape((bx,) + plane, BF16),
            shape((4, bx, by), F32),
        ),
        in_specs=[smem] * 4 + [vmem] * 2,
        out_specs=(vmem,) * 4,
        scratch_shapes=[
            pltpu.VMEM((2, 2 * bx) + plane, F32),
            pltpu.VMEM((2, 2 * bx, 8, by), F32),
            pltpu.VMEM((2, depth * bx, by), F32),
        ],
        compiler_params=pltpu.CompilerParams(vmem_limit_bytes=40 * 2**20),
        name="blend",
    )(
        block_counts,
        offset_x.reshape(slots, 1),
        offset_y.reshape(slots, 1),
        patch_wx.reshape(slots, bx).astype(F32),
        patches.reshape(slots, depth * bx, by),
        patch_wy,
    )
    n_copies = CHUNKS + 1 + 8 + 4 + 1 + CHUNKS + 4 + 8 * (PASSES - 1)
    scratch = [
        ((2, 3, bx + 4) + plane, F32),
        ((bx + 2,) + plane, F32),
        ((bx + 2,) + plane, F32),
        ((8, bx) + plane, F32),
        ((3, bx) + plane, F32),
        ((bx + 2,) + plane, F32),
        ((depth * bx, by), F32),
        ((bx + 2,) + plane, F32),
        ((5,) + plane, F32),
        ((4,) + plane, F32),
        ((2,) + plane, F32),
        ((bx, by), F32),
        ((bx, 2) + plane, BF16),
        ((2, bx, by), F32),
        ((bx,) + plane, BF16),
        ((bx, by), F32),
        ((bx,) + plane, BF16),
        ((bx, by), F32),
        ((PASSES, 2, 3, 2) + plane, BF16),
        ((PASSES, 2, 3, 2) + plane, BF16),
        ((PASSES, 3) + plane, BF16),
        ((PASSES, 2, 3) + plane, BF16),
        ((PASSES, 4, 2) + plane, BF16),
        ((2, 2) + plane, BF16),
        ((2, 2) + plane, BF16),
        ((2,) + plane, BF16),
        ((2, 2) + plane, BF16),
        ((2,) + plane, BF16),
        ((2,) + plane, BF16),
        (plane, BF16),
        ((2,) + plane, BF16),
    ]
    joined, field = pl.pallas_call(
        relax_kernel,
        out_shape=(shape((depth * bx, by), BF16), shape((3, depth * bx, by), F32)),
        in_specs=[vmem] * 8,
        out_specs=(vmem, vmem),
        scratch_shapes=[pltpu.VMEM(dims, kind) for dims, kind in scratch]
        + [pltpu.SemaphoreType.DMA((n_copies,)), pltpu.SemaphoreType.DMA((n_copies,))],
        compiler_params=pltpu.CompilerParams(
            collective_id=0, has_side_effects=True, vmem_limit_bytes=50 * 2**20
        ),
        name="relax",
    )(
        *quads,
        template.reshape(depth * bx, by),
        stiff_mu.reshape(depth * bx, by),
        stiff_lam.reshape(depth * bx, by),
        start_field.reshape(3, depth * bx, by),
    )
    return joined.reshape(depth, bx, by), field.reshape(3, depth, bx, by)


def solution(mesh):
    placed = (
        P(None, None, "gx", "gy"),
        P(None, "gy", "gx"),
        P(None, "gx", "gy"),
        P(None, "gx", "gy"),
        P(None, "gx", "gy"),
        P("gx", "gy"),
        P(None, "gx", "gy"),
        P(None, "gx", "gy"),
        P(None, "gx", "gy"),
        P(None, None, "gx", "gy"),
    )
    return jax.shard_map(
        per_device,
        mesh=mesh,
        in_specs=placed,
        out_specs=(P(None, "gx", "gy"), P(None, None, "gx", "gy")),
        check_vma=False,
    )
```

```python
import functools

import jax
import jax.numpy as jnp
from jax import lax
from jax.experimental import pallas as pl
from jax.experimental.pallas import tpu as pltpu
from jax.sharding import PartitionSpec as P

PASSES = 4
RELAX_FACTOR = 0.9
F32 = jnp.float32
BF16 = jnp.bfloat16
MESH = pl.DeviceIdType.MESH
DIRS = ((1, 0), (-1, 0), (0, 1), (0, -1), (1, 1), (1, -1), (-1, 1), (-1, -1))
CHUNKS = 4
GROUP = 8


def blend_kernel(count, table, patches, wy_ref, q00, qx, q01, wout, canvas, wcan, res, held, arrived):
    by = held.shape[-1]
    bx, depth = q00.shape[:2]
    live = count[0, 0]

    def fetch(s):
        return pltpu.make_async_copy(patches.at[s], held.at[s], arrived.at[s])

    def begin(s, carry):
        fetch(s).start()
        return carry

    lax.fori_loop(0, live, begin, 0)
    canvas[...] = jnp.zeros_like(canvas)
    wcan[...] = jnp.zeros_like(wcan)
    source = lax.broadcasted_iota(jnp.int32, (by, 2 * by), 0)
    target = lax.broadcasted_iota(jnp.int32, (by, 2 * by), 1)

    def add_patch(s, carry):
        ox = table[s, 0].astype(jnp.int32)
        oy = table[s, 1].astype(jnp.int32)
        place = jnp.where(target == source + oy, 1.0, 0.0).astype(BF16)
        fetch(s).wait()
        moved = jnp.dot(held[s], place, preferred_element_type=F32)
        res[0] = moved[:, :by]
        res[1] = moved[:, by:]
        along_y = jnp.broadcast_to(wy_ref[s].astype(F32), (16, by)).astype(BF16)
        wy_row = jnp.dot(along_y, place, preferred_element_type=F32)[:8]
        for x in range(bx):
            wx = table[s, 2 + x]
            for h in range(2):
                weight = wx * wy_row[:, h * by : (h + 1) * by]
                canvas[h, ox + x] += res[h, pl.ds(x, depth, stride=bx), :] * weight[0:1]
                wcan[h, ox + x] += weight
        return carry

    lax.fori_loop(0, live, add_patch, 0)
    q00[...] = canvas[0, :bx]
    qx[:, 0] = canvas[0, bx:].astype(BF16)
    qx[:, 1] = canvas[1, bx:].astype(BF16)
    q01[...] = canvas[1, :bx].astype(BF16)
    for x in range(bx):
        wout[0, x : x + 1] = wcan[0, x, 0:1]
        wout[1, x : x + 1] = wcan[0, bx + x, 0:1]
        wout[2, x : x + 1] = wcan[1, bx + x, 0:1]
        wout[3, x : x + 1] = wcan[1, x, 0:1]


def relax_kernel(
    q00, qx, q01, wq, tmpl, mu_ref, lam_ref, fld, jout, fout,
    field, mu, qb, coef, force, joined, tall, grad, acc, packed, cpack, wsum,
    land_q, land_w, sy, sw, land_y, land_wy,
    xs, xl, ap, al, dl, cxs, cxl, cap, cal, jxs, jxl, jap, jal,
    send_sem, recv_sem,
):
    bx, depth, by = q00.shape
    gx, gy = lax.axis_index("gx"), lax.axis_index("gy")
    nx, ny = lax.axis_size("gx"), lax.axis_size("gy")

    def exists(d):
        ok = True
        for where, step, count in ((gx, d[0], nx), (gy, d[1], ny)):
            if step == 1:
                ok = jnp.logical_and(ok, where < count - 1)
            if step == -1:
                ok = jnp.logical_and(ok, where > 0)
        return ok

    def opposite(d):
        return (-d[0], -d[1])

    pending = []

    def rdma(src, dst, idx, d):
        return pltpu.make_async_remote_copy(
            src_ref=src, dst_ref=dst, send_sem=send_sem.at[idx], recv_sem=recv_sem.at[idx],
            device_id=(gx + d[0], gy + d[1]), device_id_type=MESH,
        )

    counter = [0]

    def send(src, dst, d):
        idx = counter[0]
        counter[0] += 1

        @pl.when(exists(d))
        def _():
            rdma(src, dst, idx, d).start()

        pending.append((src, dst, idx, d))

        def arrive():
            @pl.when(exists(opposite(d)))
            def _():
                rdma(src, dst, idx, d).wait_recv()

        return arrive

    lane = lax.broadcasted_iota(jnp.int32, (depth, by), 1)
    level = lax.broadcasted_iota(jnp.int32, (depth, by), 0)
    pos = lax.rem(lane, GROUP)

    def strided(x):
        return pl.ds(x, depth, stride=bx)

    def z_next(v):
        return jnp.where(level == depth - 1, 0.0, pltpu.roll(v, depth - 1, 0))

    def z_prev(v):
        return jnp.where(level == 0, 0.0, pltpu.roll(v, 1, 0))

    def y_next(v, edge):
        return jnp.where(lane == by - 1, edge, pltpu.roll(v, by - 1, 1))

    def y_prev(v, edge):
        return jnp.where(lane == 0, edge, pltpu.roll(v, 1, 1))

    def at_edge(pack, x):
        return pltpu.roll(pack, by - 4 - GROUP * x, 1)

    def pack_in(slot, planes, x0):
        out = acc[slot]
        for u, plane in enumerate(planes):
            at = GROUP * (x0 + u)
            own = jnp.logical_and(lane >= at, lane < at + 4)
            out = jnp.where(own, pltpu.roll(plane, (at + 2) % by, 1), out)
        acc[slot] = out

    def pairs(low, high, body):
        def two(n, carry):
            body(2 * n)
            return carry

        lax.fori_loop(low // 2, high // 2, two, 0)

    def merge(own, left, right):
        left, right = left.astype(F32), right.astype(F32)
        out = jnp.where(pos >= 6, pltpu.roll(own, 4, 1), own)
        out = jnp.where(pos == 2, pltpu.roll(left, 2, 1), out)
        out = jnp.where(pos == 4, pltpu.roll(left, 3, 1), out)
        out = jnp.where(pos == 3, pltpu.roll(right, 1, 1), out)
        return jnp.where(pos == 5, pltpu.roll(right, 2, 1), out)

    barrier = pltpu.get_barrier_semaphore()
    total = 0
    for d in DIRS:
        @pl.when(exists(d))
        def _(d=d):
            pl.semaphore_signal(barrier, inc=1, device_id=(gx + d[0], gy + d[1]), device_id_type=MESH)

        total = total + jnp.where(exists(d), 1, 0)
    pl.semaphore_wait(barrier, total)

    step = bx // CHUNKS
    got_q = []
    for c in range(CHUNKS):
        part = pl.ds(c * step, step)
        got_q.append(send(qx.at[part], land_q.at[part], (1, 0)))
    got_w = send(wq.at[pl.ds(1, 2)], land_w, (1, 0))

    for k, d in enumerate(DIRS):
        @pl.when(jnp.logical_not(exists(opposite(d))))
        def _(k=k):
            if k == 0:
                land_q[...] = jnp.zeros_like(land_q)
                land_w[...] = jnp.zeros_like(land_w)
            if k == 2:
                land_y[...] = jnp.zeros_like(land_y)
                land_wy[...] = jnp.zeros_like(land_wy)
            if k < 2:
                for p in range(PASSES):
                    xl[p, k] = jnp.zeros(xl.shape[2:], BF16)
                cxl[k] = jnp.zeros(cxl.shape[1:], BF16)
                jxl[k] = jnp.zeros(jxl.shape[1:], BF16)
            elif k < 4:
                for p in range(PASSES):
                    al[p, k - 2] = jnp.zeros(al.shape[2:], BF16)
                cal[k - 2] = jnp.zeros(cal.shape[1:], BF16)
                jal[k - 2] = jnp.zeros(jal.shape[1:], BF16)
            else:
                for p in range(PASSES):
                    dl[p, k - 4] = jnp.zeros(dl.shape[2:], BF16)

    acc[...] = jnp.zeros_like(acc)

    def load(x0):
        span = (x0, x0 + 1)
        planes = [[fld[c, strided(x), :] for x in span] for c in range(3)]
        mus = [mu_ref[strided(x), :] for x in span]
        bulks = [lam_ref[strided(x), :] + one for x, one in zip(span, mus)]
        for u, x in enumerate(span):
            for c in range(3):
                field[0, c, x + 2] = planes[c][u]
            mu[x + 1] = mus[u]
            qb[x + 1] = bulks[u]
        for slot, values in enumerate(planes + [mus, bulks]):
            pack_in(slot, values, x0)

    pairs(0, bx, load)

    def send_planes(p, b):
        for c in range(3):
            xs[p, 0, c] = field[b, c, bx : bx + 2].astype(BF16)
            xs[p, 1, c] = field[b, c, 2:4].astype(BF16)
        return [send(xs.at[p, k], xl.at[p, k], DIRS[k]) for k in range(2)]

    def send_packs(p):
        for c in range(3):
            ap[p, c] = acc[c].astype(BF16)
        far = [send(ap.at[p, pl.ds(1, 2)], dl.at[p, k - 4], DIRS[k]) for k in range(4, 8)]
        near = [send(ap.at[p], al.at[p, k - 2], DIRS[k]) for k in range(2, 4)]
        return near, far

    got_planes = send_planes(0, 0)
    got_packs = send_packs(0)
    for k, at in ((0, bx), (1, 1)):
        cxs[k, 0] = mu[at].astype(BF16)
        cxs[k, 1] = qb[at].astype(BF16)
    cap[...] = acc[3:5].astype(BF16)
    got_coef = [send(cxs.at[k], cxl.at[k], DIRS[k]) for k in range(2)]
    got_coef += [send(cap, cal.at[k - 2], DIRS[k]) for k in range(2, 4)]

    got_w()
    sw[...] = wq[3] + land_w[1]
    got_wy = send(sw, land_wy, (0, 1))
    got_y = []
    for c in range(CHUNKS):
        part = pl.ds(c * step, step)
        got_q[c]()
        sy[part] = (q01[part].astype(F32) + land_q[part, 1].astype(F32)).astype(BF16)
        got_y.append(send(sy.at[part], land_y.at[part], (0, 1)))

    for arrive in got_coef:
        arrive()
    for k, at in ((0, 0), (1, bx + 1)):
        mu[at] = cxl[k, 0].astype(F32)
        qb[at] = cxl[k, 1].astype(F32)
    for c in range(2):
        cpack[c] = merge(acc[3 + c], cal[0, c], cal[1, c])
    cpack[1] = 0.25 * cpack[1]

    def coefficients(x0):
        found = []
        for x in (x0, x0 + 1):
            here = mu[x + 1]
            rate = RELAX_FACTOR / (6.0 * here + 3.0 * qb[x + 1])
            half = 0.5 * rate
            edge = at_edge(cpack[0], x)
            near = (
                z_next(here), z_prev(here), mu[x + 2], mu[x], y_next(here, edge), y_prev(here, edge),
            )
            values = [half * (here + other) for other in near]
            rest = 1.0
            for one in values:
                rest = rest - one
            found.append(values + [rest, rate])
        for u in range(2):
            for n in range(8):
                coef[n, x0 + u] = found[u][n]

    pairs(0, bx, coefficients)

    def scale(x, carry):
        qb[x] = 0.25 * qb[x]
        return carry

    lax.fori_loop(0, bx + 2, scale, 0)

    def relax(p, got_planes, got_packs):
        b, nb = p % 2, 1 - p % 2
        last = p == PASSES - 1
        for arrive in got_packs[0]:
            arrive()
        for c in range(3):
            packed[c] = merge(acc[c], al[p, 0, c], al[p, 1, c])

        def gradient(at, edge):
            vz, vy = field[b, 0, at + 1], field[b, 2, at + 1]
            return qb[at] * (
                (field[b, 1, at + 2] - field[b, 1, at])
                + (z_next(vz) - z_prev(vz))
                + (y_next(vy, edge) - y_prev(vy, edge))
            )

        def inner(x0):
            pack = packed[2]
            values = [gradient(x0 + u + 1, at_edge(pack, x0 + u)) for u in range(2)]
            for u in range(2):
                grad[x0 + u + 1] = values[u]

        pairs(2, bx - 2, inner)
        for arrive in got_planes:
            arrive()
        for c in range(3):
            field[b, c, 0:2] = xl[p, 0, c].astype(F32)
            field[b, c, bx + 2 : bx + 4] = xl[p, 1, c].astype(F32)
        inner(0)
        inner(bx - 2)
        for arrive in got_packs[1]:
            arrive()
        corner = [[dl[p, k, c].astype(F32) for c in range(2)] for k in range(4)]
        top = GROUP * (bx - 1)

        def bring(k, c, at):
            plus_x, plus_y = DIRS[4 + k]
            source = (top if plus_x == 1 else 0) + (1 if plus_y == 1 else 2)
            return pltpu.roll(corner[k][c], (at - source) % by, 1)

        def edge_corners(low, high):
            return jnp.where(lane == 0, bring(low, 1, 0), bring(high, 1, by - 1))

        vx = packed[1]
        ahead = pltpu.roll(vx, by - GROUP, 1)
        ahead = jnp.where(lane == top + 3, bring(3, 0, top + 3), ahead)
        ahead = jnp.where(lane == top + 4, bring(2, 0, top + 4), ahead)
        behind = pltpu.roll(vx, GROUP, 1)
        behind = jnp.where(lane == 3, bring(1, 0, 3), behind)
        behind = jnp.where(lane == 4, bring(0, 0, 4), behind)
        if GROUP * bx < by:
            ahead = jnp.where(lane >= GROUP * bx, 0.0, ahead)
        vz, vy = packed[0], packed[2]
        packed[3] = cpack[1] * (
            (ahead - behind) + (z_next(vz) - z_prev(vz))
            + (pltpu.roll(vy, by - 2, 1) - pltpu.roll(vy, 2, 1))
        )

        low = gradient(0, edge_corners(0, 1))
        high = gradient(bx + 1, edge_corners(2, 3))
        grad[0] = low
        grad[bx + 1] = high
        if not last:
            acc[0:3] = jnp.zeros((3, depth, by), F32)

        def update(x0):
            news = [[], [], []]
            for x in (x0, x0 + 1):
                g = grad[x + 1]
                g_edge = at_edge(packed[3], x)
                rise = (
                    z_next(g) - z_prev(g),
                    grad[x + 2] - grad[x],
                    y_next(g, g_edge) - y_prev(g, g_edge),
                )
                k = [coef[n, x] for n in range(8)]
                for c in range(3):
                    v = field[b, c, x + 2]
                    edge = at_edge(packed[c], x)
                    new = k[6] * v + k[7] * rise[c]
                    new = new + k[0] * z_next(v) + k[1] * z_prev(v)
                    new = new + k[2] * field[b, c, x + 3] + k[3] * field[b, c, x + 1]
                    new = new + k[4] * y_next(v, edge) + k[5] * y_prev(v, edge)
                    if p > 0:
                        new = new + force[c, x]
                    news[c].append(new)
            for c in range(3):
                for u in range(2):
                    if last:
                        fout[c, strided(x0 + u), :] = news[c][u]
                    else:
                        field[nb, c, x0 + u + 2] = news[c][u]
                if p > 0 and not last:
                    pack_in(c, news[c], x0)

        if p == 0 or last:
            pairs(0, bx, update)
            return None
        update(0)
        update(bx - 2)
        got_planes = send_planes(p + 1, nb)
        pairs(2, bx - 2, update)
        return got_planes, send_packs(p + 1)

    relax(0, got_planes, got_packs)

    got_wy()
    wsum[...] = jnp.maximum(wq[0] + land_w[0] + land_wy[...], 1.0)
    acc[3] = jnp.zeros((depth, by), F32)
    tall[...] = tmpl[...].astype(F32)

    def join(x0):
        planes = []
        for x in (x0, x0 + 1):
            value = q00[x] + land_q[x, 0].astype(F32) + land_y[x].astype(F32)
            planes.append((value / wsum[pl.ds(x, 1), :]).astype(BF16).astype(F32))
        for u in range(2):
            joined[x0 + u + 1] = planes[u]
        pack_in(3, planes, x0)

    for c in range(CHUNKS):
        got_y[c]()
        pairs(c * step, (c + 1) * step, join)
    jxs[0] = joined[bx].astype(BF16)
    jxs[1] = joined[1].astype(BF16)
    jap[...] = acc[3].astype(BF16)
    got = [send(jxs.at[k], jxl.at[k], DIRS[k]) for k in range(2)]
    got += [send(jap, jal.at[k - 2], DIRS[k]) for k in range(2, 4)]
    for arrive in got:
        arrive()
    joined[0] = jxl[0].astype(F32)
    joined[bx + 1] = jxl[1].astype(F32)
    cpack[0] = merge(acc[3], jal[0], jal[1])

    def forcing(x0):
        span = (x0, x0 + 1)
        ones, news, heres = [[], [], []], [[], [], []], []
        for x in span:
            here = joined[x + 1]
            edge = at_edge(cpack[0], x)
            mismatch = (tall[strided(x), :] - here) * 0.5 * coef[7, x]
            slopes = (
                z_next(here) - z_prev(here),
                joined[x + 2] - joined[x],
                y_next(here, edge) - y_prev(here, edge),
            )
            heres.append(here)
            for c in range(3):
                ones[c].append(mismatch * slopes[c])
                news[c].append(field[1, c, x + 2] + ones[c][-1])
        for u, x in enumerate(span):
            tall[strided(x), :] = heres[u]
            for c in range(3):
                force[c, x] = ones[c][u]
                field[1, c, x + 2] = news[c][u]
        for c in range(3):
            pack_in(c, news[c], x0)

    forcing(0)
    forcing(bx - 2)
    got_planes = send_planes(1, 1)
    pairs(2, bx - 2, forcing)
    got_packs = send_packs(1)
    jout[...] = tall[...].astype(BF16)
    for p in range(1, PASSES):
        sent = relax(p, got_planes, got_packs)
        if sent is not None:
            got_planes, got_packs = sent
    for src, dst, idx, d in pending:
        @pl.when(exists(d))
        def _(src=src, dst=dst, idx=idx, d=d):
            rdma(src, dst, idx, d).wait_send()


def per_device(
    patches, patch_wx, patch_wy, offset_x, offset_y, block_counts, template, stiff_mu, stiff_lam, start_field
):
    slots, depth, bx, by = patches.shape
    vmem = pl.BlockSpec(memory_space=pltpu.VMEM)
    smem = pl.BlockSpec(memory_space=pltpu.SMEM)
    plane = (depth, by)
    shape = jax.ShapeDtypeStruct
    table = jnp.concatenate(
        [part.reshape(slots, -1).astype(F32) for part in (offset_x, offset_y, patch_wx)], axis=1
    )
    quads = pl.pallas_call(
        blend_kernel,
        out_shape=(
            shape((bx,) + plane, F32),
            shape((bx, 2) + plane, BF16),
            shape((bx,) + plane, BF16),
            shape((4, bx, by), F32),
        ),
        in_specs=[smem] * 2 + [pl.BlockSpec(memory_space=pltpu.HBM), vmem],
        out_specs=(vmem,) * 4,
        scratch_shapes=[
            pltpu.VMEM((2, 2 * bx) + plane, F32),
            pltpu.VMEM((2, 2 * bx, 8, by), F32),
            pltpu.VMEM((2, depth * bx, by), F32),
            pltpu.VMEM((slots, depth * bx, by), BF16),
            pltpu.SemaphoreType.DMA((slots,)),
        ],
        compiler_params=pltpu.CompilerParams(vmem_limit_bytes=40 * 2**20),
        name="blend",
    )(
        block_counts,
        table,
        patches.reshape(slots, depth * bx, by),
        patch_wy,
    )
    n_copies = CHUNKS + 1 + 8 + 4 + 1 + CHUNKS + 4 + 8 * (PASSES - 1)
    scratch = [
        ((2, 3, bx + 4) + plane, F32),
        ((bx + 2,) + plane, F32),
        ((bx + 2,) + plane, F32),
        ((8, bx) + plane, F32),
        ((3, bx) + plane, F32),
        ((bx + 2,) + plane, F32),
        ((depth * bx, by), F32),
        ((bx + 2,) + plane, F32),
        ((5,) + plane, F32),
        ((4,) + plane, F32),
        ((2,) + plane, F32),
        ((bx, by), F32),
        ((bx, 2) + plane, BF16),
        ((2, bx, by), F32),
        ((bx,) + plane, BF16),
        ((bx, by), F32),
        ((bx,) + plane, BF16),
        ((bx, by), F32),
        ((PASSES, 2, 3, 2) + plane, BF16),
        ((PASSES, 2, 3, 2) + plane, BF16),
        ((PASSES, 3) + plane, BF16),
        ((PASSES, 2, 3) + plane, BF16),
        ((PASSES, 4, 2) + plane, BF16),
        ((2, 2) + plane, BF16),
        ((2, 2) + plane, BF16),
        ((2,) + plane, BF16),
        ((2, 2) + plane, BF16),
        ((2,) + plane, BF16),
        ((2,) + plane, BF16),
        (plane, BF16),
        ((2,) + plane, BF16),
    ]
    joined, field = pl.pallas_call(
        relax_kernel,
        out_shape=(shape((depth * bx, by), BF16), shape((3, depth * bx, by), F32)),
        in_specs=[vmem] * 8,
        out_specs=(vmem, vmem),
        scratch_shapes=[pltpu.VMEM(dims, kind) for dims, kind in scratch]
        + [pltpu.SemaphoreType.DMA((n_copies,)), pltpu.SemaphoreType.DMA((n_copies,))],
        compiler_params=pltpu.CompilerParams(
            collective_id=0, has_side_effects=True, vmem_limit_bytes=50 * 2**20
        ),
        name="relax",
    )(
        *quads,
        template.reshape(depth * bx, by),
        stiff_mu.reshape(depth * bx, by),
        stiff_lam.reshape(depth * bx, by),
        start_field.reshape(3, depth * bx, by),
    )
    return joined.reshape(depth, bx, by), field.reshape(3, depth, bx, by)


def solution(mesh):
    placed = (
        P(None, None, "gx", "gy"),
        P(None, "gy", "gx"),
        P(None, "gx", "gy"),
        P(None, "gx", "gy"),
        P(None, "gx", "gy"),
        P("gx", "gy"),
        P(None, "gx", "gy"),
        P(None, "gx", "gy"),
        P(None, "gx", "gy"),
        P(None, None, "gx", "gy"),
    )
    return jax.shard_map(
        per_device,
        mesh=mesh,
        in_specs=placed,
        out_specs=(P(None, "gx", "gy"), P(None, None, "gx", "gy")),
        check_vma=False,
    )
```

```python
import functools

import jax
import jax.numpy as jnp
from jax import lax
from jax.experimental import pallas as pl
from jax.experimental.pallas import tpu as pltpu
from jax.sharding import PartitionSpec as P

PASSES = 4
RELAX_FACTOR = 0.9
F32 = jnp.float32
BF16 = jnp.bfloat16
MESH = pl.DeviceIdType.MESH
DIRS = ((1, 0), (-1, 0), (0, 1), (0, -1), (1, 1), (1, -1), (-1, 1), (-1, -1))
CHUNKS = 4
GROUP = 8


def blend_kernel(count, ox_ref, oy_ref, patches, wx_ref, wy_ref, q00, qx, q01, wout, canvas, wcan, res, held, wxf, wyf, arrived):
    by = held.shape[-1]
    bx, depth = q00.shape[:2]
    live = count[0, 0]

    def fetch(s):
        return pltpu.make_async_copy(patches.at[s], held.at[s], arrived.at[s])

    def begin(s, carry):
        fetch(s).start()
        return carry

    lax.fori_loop(0, live, begin, 0)
    canvas[...] = jnp.zeros_like(canvas)
    wcan[...] = jnp.zeros_like(wcan)
    wxf[...] = wx_ref[...].astype(F32)
    wyf[...] = wy_ref[...].astype(F32)
    source = lax.broadcasted_iota(jnp.int32, (by, 2 * by), 0)
    target = lax.broadcasted_iota(jnp.int32, (by, 2 * by), 1)

    def add_patch(s, carry):
        ox = ox_ref[0, s]
        place = jnp.where(target == source + oy_ref[0, s], 1.0, 0.0).astype(BF16)
        fetch(s).wait()
        moved = jnp.dot(held[s], place, preferred_element_type=F32)
        res[0] = moved[:, :by]
        res[1] = moved[:, by:]
        along_y = jnp.broadcast_to(wyf[pl.ds(s, 1), :], (16, by)).astype(BF16)
        wy_row = jnp.dot(along_y, place, preferred_element_type=F32)[:8]
        along_x = jnp.broadcast_to(wxf[pl.ds(s, 1), :], (8, bx))
        for x0 in range(0, bx, 4):
            for h in range(2):
                span = range(x0, x0 + 4)
                weights = [along_x[:, x : x + 1] * wy_row[:, h * by : (h + 1) * by] for x in span]
                sums = [
                    canvas[h, ox + x] + res[h, pl.ds(x, depth, stride=bx), :] * weight[0:1]
                    for x, weight in zip(span, weights)
                ]
                totals = [wcan[h, ox + x] + weight for x, weight in zip(span, weights)]
                for n, x in enumerate(span):
                    canvas[h, ox + x] = sums[n]
                    wcan[h, ox + x] = totals[n]
        return carry

    lax.fori_loop(0, live, add_patch, 0)
    q00[...] = canvas[0, :bx]
    qx[:, 0] = canvas[0, bx:].astype(BF16)
    qx[:, 1] = canvas[1, bx:].astype(BF16)
    q01[...] = canvas[1, :bx].astype(BF16)
    for x in range(bx):
        wout[0, x : x + 1] = wcan[0, x, 0:1]
        wout[1, x : x + 1] = wcan[0, bx + x, 0:1]
        wout[2, x : x + 1] = wcan[1, bx + x, 0:1]
        wout[3, x : x + 1] = wcan[1, x, 0:1]


def relax_kernel(
    q00, qx, q01, wq, tmpl, mu_ref, lam_ref, fld, jout, fout,
    field, mu, qb, coef, force, joined, tall, grad, acc, packed, cpack, wsum,
    land_q, land_w, sy, sw, land_y, land_wy,
    xs, xl, ap, al, dl, cxs, cxl, cap, cal, jxs, jxl, jap, jal,
    send_sem, recv_sem,
):
    bx, depth, by = q00.shape
    gx, gy = lax.axis_index("gx"), lax.axis_index("gy")
    nx, ny = lax.axis_size("gx"), lax.axis_size("gy")

    def exists(d):
        ok = True
        for where, step, count in ((gx, d[0], nx), (gy, d[1], ny)):
            if step == 1:
                ok = jnp.logical_and(ok, where < count - 1)
            if step == -1:
                ok = jnp.logical_and(ok, where > 0)
        return ok

    def opposite(d):
        return (-d[0], -d[1])

    pending = []

    def rdma(src, dst, idx, d):
        return pltpu.make_async_remote_copy(
            src_ref=src, dst_ref=dst, send_sem=send_sem.at[idx], recv_sem=recv_sem.at[idx],
            device_id=(gx + d[0], gy + d[1]), device_id_type=MESH,
        )

    counter = [0]

    def send(src, dst, d):
        idx = counter[0]
        counter[0] += 1

        @pl.when(exists(d))
        def _():
            rdma(src, dst, idx, d).start()

        pending.append((src, dst, idx, d))

        def arrive():
            @pl.when(exists(opposite(d)))
            def _():
                rdma(src, dst, idx, d).wait_recv()

        return arrive

    lane = lax.broadcasted_iota(jnp.int32, (depth, by), 1)
    level = lax.broadcasted_iota(jnp.int32, (depth, by), 0)
    pos = lax.rem(lane, GROUP)

    def strided(x):
        return pl.ds(x, depth, stride=bx)

    def z_next(v):
        return jnp.where(level == depth - 1, 0.0, pltpu.roll(v, depth - 1, 0))

    def z_prev(v):
        return jnp.where(level == 0, 0.0, pltpu.roll(v, 1, 0))

    def y_next(v, edge):
        return jnp.where(lane == by - 1, edge, pltpu.roll(v, by - 1, 1))

    def y_prev(v, edge):
        return jnp.where(lane == 0, edge, pltpu.roll(v, 1, 1))

    def at_edge(pack, x):
        return pltpu.roll(pack, by - 4 - GROUP * x, 1)

    def pack_in(slot, planes, x0):
        out = acc[slot]
        for u, plane in enumerate(planes):
            at = GROUP * (x0 + u)
            own = jnp.logical_and(lane >= at, lane < at + 4)
            out = jnp.where(own, pltpu.roll(plane, (at + 2) % by, 1), out)
        acc[slot] = out

    def pairs(low, high, body):
        def two(n, carry):
            body(2 * n)
            return carry

        lax.fori_loop(low // 2, high // 2, two, 0)

    def merge(own, left, right):
        left, right = left.astype(F32), right.astype(F32)
        out = jnp.where(pos >= 6, pltpu.roll(own, 4, 1), own)
        out = jnp.where(pos == 2, pltpu.roll(left, 2, 1), out)
        out = jnp.where(pos == 4, pltpu.roll(left, 3, 1), out)
        out = jnp.where(pos == 3, pltpu.roll(right, 1, 1), out)
        return jnp.where(pos == 5, pltpu.roll(right, 2, 1), out)

    barrier = pltpu.get_barrier_semaphore()
    total = 0
    for d in DIRS:
        @pl.when(exists(d))
        def _(d=d):
            pl.semaphore_signal(barrier, inc=1, device_id=(gx + d[0], gy + d[1]), device_id_type=MESH)

        total = total + jnp.where(exists(d), 1, 0)

    for k, d in enumerate(DIRS):
        @pl.when(jnp.logical_not(exists(opposite(d))))
        def _(k=k):
            if k == 0:
                land_q[...] = jnp.zeros_like(land_q)
                land_w[...] = jnp.zeros_like(land_w)
            if k == 2:
                land_y[...] = jnp.zeros_like(land_y)
                land_wy[...] = jnp.zeros_like(land_wy)
            if k < 2:
                for p in range(PASSES):
                    xl[p, k] = jnp.zeros(xl.shape[2:], BF16)
                cxl[k] = jnp.zeros(cxl.shape[1:], BF16)
                jxl[k] = jnp.zeros(jxl.shape[1:], BF16)
            elif k < 4:
                for p in range(PASSES):
                    al[p, k - 2] = jnp.zeros(al.shape[2:], BF16)
                cal[k - 2] = jnp.zeros(cal.shape[1:], BF16)
                jal[k - 2] = jnp.zeros(jal.shape[1:], BF16)
            else:
                for p in range(PASSES):
                    dl[p, k - 4] = jnp.zeros(dl.shape[2:], BF16)

    acc[...] = jnp.zeros_like(acc)
    pl.semaphore_wait(barrier, total)

    step = bx // CHUNKS
    got_q = []
    for c in range(CHUNKS):
        part = pl.ds(c * step, step)
        got_q.append(send(qx.at[part], land_q.at[part], (1, 0)))
    got_w = send(wq.at[pl.ds(1, 2)], land_w, (1, 0))

    def load(x0):
        span = (x0, x0 + 1)
        planes = [[fld[c, strided(x), :] for x in span] for c in range(3)]
        mus = [mu_ref[strided(x), :] for x in span]
        bulks = [0.25 * (lam_ref[strided(x), :] + one) for x, one in zip(span, mus)]
        for u, x in enumerate(span):
            for c in range(3):
                field[0, c, x + 2] = planes[c][u]
            mu[x + 1] = mus[u]
            qb[x + 1] = bulks[u]
        for slot, values in enumerate(planes + [mus, bulks]):
            pack_in(slot, values, x0)

    pairs(0, bx, load)

    def send_planes(p, b):
        for c in range(3):
            xs[p, 0, c] = field[b, c, bx : bx + 2].astype(BF16)
            xs[p, 1, c] = field[b, c, 2:4].astype(BF16)
        return [send(xs.at[p, k], xl.at[p, k], DIRS[k]) for k in range(2)]

    def send_packs(p):
        for c in range(3):
            ap[p, c] = acc[c].astype(BF16)
        far = [send(ap.at[p, pl.ds(1, 2)], dl.at[p, k - 4], DIRS[k]) for k in range(4, 8)]
        near = [send(ap.at[p], al.at[p, k - 2], DIRS[k]) for k in range(2, 4)]
        return near, far

    got_planes = send_planes(0, 0)
    got_packs = send_packs(0)
    for k, at in ((0, bx), (1, 1)):
        cxs[k, 0] = mu[at].astype(BF16)
        cxs[k, 1] = qb[at].astype(BF16)
    cap[...] = acc[3:5].astype(BF16)
    got_coef = [send(cxs.at[k], cxl.at[k], DIRS[k]) for k in range(2)]
    got_coef += [send(cap, cal.at[k - 2], DIRS[k]) for k in range(2, 4)]

    got_w()
    sw[...] = wq[3] + land_w[1]
    got_wy = send(sw, land_wy, (0, 1))
    got_y = []

    def pass_on(c):
        part = pl.ds(c * step, step)
        got_q[c]()
        sy[part] = (q01[part].astype(F32) + land_q[part, 1].astype(F32)).astype(BF16)
        got_y.append(send(sy.at[part], land_y.at[part], (0, 1)))

    for c in range(CHUNKS // 2):
        pass_on(c)

    for arrive in got_coef:
        arrive()
    for k, at in ((0, 0), (1, bx + 1)):
        mu[at] = cxl[k, 0].astype(F32)
        qb[at] = cxl[k, 1].astype(F32)
    for c in range(2):
        cpack[c] = merge(acc[3 + c], cal[0, c], cal[1, c])

    def coefficients(x0):
        found = []
        for x in (x0, x0 + 1):
            here = mu[x + 1]
            rate = RELAX_FACTOR / (6.0 * here + 12.0 * qb[x + 1])
            half = 0.5 * rate
            edge = at_edge(cpack[0], x)
            near = (
                z_next(here), z_prev(here), mu[x + 2], mu[x], y_next(here, edge), y_prev(here, edge),
            )
            values = [half * (here + other) for other in near]
            rest = 1.0
            for one in values:
                rest = rest - one
            found.append(values + [rest, rate])
        for u in range(2):
            for n in range(8):
                coef[n, x0 + u] = found[u][n]

    pairs(0, bx, coefficients)
    for c in range(CHUNKS // 2, CHUNKS):
        pass_on(c)

    def relax(p, got_planes, got_packs):
        b, nb = p % 2, 1 - p % 2
        last = p == PASSES - 1
        for arrive in got_packs[0]:
            arrive()
        for c in range(3):
            packed[c] = merge(acc[c], al[p, 0, c], al[p, 1, c])

        def gradient(at, edge):
            vz, vy = field[b, 0, at + 1], field[b, 2, at + 1]
            return qb[at] * (
                (field[b, 1, at + 2] - field[b, 1, at])
                + (z_next(vz) - z_prev(vz))
                + (y_next(vy, edge) - y_prev(vy, edge))
            )

        def inner(span):
            pack = packed[2]
            values = [gradient(x + 1, at_edge(pack, x)) for x in span]
            for x, value in zip(span, values):
                grad[x + 1] = value

        def four(n, carry):
            inner([2 + 4 * n + u for u in range(4)])
            return carry

        lax.fori_loop(0, (bx - 4) // 4, four, 0)
        for arrive in got_planes:
            arrive()
        for c in range(3):
            field[b, c, 0:2] = xl[p, 0, c].astype(F32)
            field[b, c, bx + 2 : bx + 4] = xl[p, 1, c].astype(F32)
        inner([0, 1, bx - 2, bx - 1])
        for arrive in got_packs[1]:
            arrive()
        corner = [[dl[p, k, c].astype(F32) for c in range(2)] for k in range(4)]
        top = GROUP * (bx - 1)

        def bring(k, c, at):
            plus_x, plus_y = DIRS[4 + k]
            source = (top if plus_x == 1 else 0) + (1 if plus_y == 1 else 2)
            return pltpu.roll(corner[k][c], (at - source) % by, 1)

        def edge_corners(low, high):
            return jnp.where(lane == 0, bring(low, 1, 0), bring(high, 1, by - 1))

        vx = packed[1]
        ahead = pltpu.roll(vx, by - GROUP, 1)
        ahead = jnp.where(lane == top + 3, bring(3, 0, top + 3), ahead)
        ahead = jnp.where(lane == top + 4, bring(2, 0, top + 4), ahead)
        behind = pltpu.roll(vx, GROUP, 1)
        behind = jnp.where(lane == 3, bring(1, 0, 3), behind)
        behind = jnp.where(lane == 4, bring(0, 0, 4), behind)
        if GROUP * bx < by:
            ahead = jnp.where(lane >= GROUP * bx, 0.0, ahead)
        vz, vy = packed[0], packed[2]
        packed[3] = cpack[1] * (
            (ahead - behind) + (z_next(vz) - z_prev(vz))
            + (pltpu.roll(vy, by - 2, 1) - pltpu.roll(vy, 2, 1))
        )

        low = gradient(0, edge_corners(0, 1))
        high = gradient(bx + 1, edge_corners(2, 3))
        grad[0] = low
        grad[bx + 1] = high
        if not last:
            acc[0:3] = jnp.zeros((3, depth, by), F32)

        def update(x0):
            news = [[], [], []]
            for x in (x0, x0 + 1):
                g = grad[x + 1]
                g_edge = at_edge(packed[3], x)
                rise = (
                    z_next(g) - z_prev(g),
                    grad[x + 2] - grad[x],
                    y_next(g, g_edge) - y_prev(g, g_edge),
                )
                k = [coef[n, x] for n in range(8)]
                for c in range(3):
                    v = field[b, c, x + 2]
                    edge = at_edge(packed[c], x)
                    new = k[6] * v + k[7] * rise[c]
                    new = new + k[0] * z_next(v) + k[1] * z_prev(v)
                    new = new + k[2] * field[b, c, x + 3] + k[3] * field[b, c, x + 1]
                    new = new + k[4] * y_next(v, edge) + k[5] * y_prev(v, edge)
                    if p > 0:
                        new = new + force[c, x]
                    news[c].append(new)
            for c in range(3):
                for u in range(2):
                    if last:
                        fout[c, strided(x0 + u), :] = news[c][u]
                    else:
                        field[nb, c, x0 + u + 2] = news[c][u]
                if p > 0 and not last:
                    pack_in(c, news[c], x0)

        if p == 0 or last:
            pairs(0, bx, update)
            return None
        update(0)
        update(bx - 2)
        got_planes = send_planes(p + 1, nb)
        pairs(2, bx - 2, update)
        return got_planes, send_packs(p + 1)

    relax(0, got_planes, got_packs)

    got_wy()
    wsum[...] = jnp.maximum(wq[0] + land_w[0] + land_wy[...], 1.0)
    acc[3] = jnp.zeros((depth, by), F32)
    tall[...] = tmpl[...].astype(F32)

    def join(x0):
        planes = []
        for x in (x0, x0 + 1):
            value = q00[x] + land_q[x, 0].astype(F32) + land_y[x].astype(F32)
            planes.append((value / wsum[pl.ds(x, 1), :]).astype(BF16).astype(F32))
        for u in range(2):
            joined[x0 + u + 1] = planes[u]
        pack_in(3, planes, x0)

    for c in range(CHUNKS):
        got_y[c]()
        pairs(c * step, (c + 1) * step, join)
    jxs[0] = joined[bx].astype(BF16)
    jxs[1] = joined[1].astype(BF16)
    jap[...] = acc[3].astype(BF16)
    got = [send(jxs.at[k], jxl.at[k], DIRS[k]) for k in range(2)]
    got += [send(jap, jal.at[k - 2], DIRS[k]) for k in range(2, 4)]
    for arrive in got:
        arrive()
    joined[0] = jxl[0].astype(F32)
    joined[bx + 1] = jxl[1].astype(F32)
    cpack[0] = merge(acc[3], jal[0], jal[1])

    def forcing(x0):
        span = (x0, x0 + 1)
        ones, news, heres = [[], [], []], [[], [], []], []
        for x in span:
            here = joined[x + 1]
            edge = at_edge(cpack[0], x)
            mismatch = (tall[strided(x), :] - here) * 0.5 * coef[7, x]
            slopes = (
                z_next(here) - z_prev(here),
                joined[x + 2] - joined[x],
                y_next(here, edge) - y_prev(here, edge),
            )
            heres.append(here)
            for c in range(3):
                ones[c].append(mismatch * slopes[c])
                news[c].append(field[1, c, x + 2] + ones[c][-1])
        for u, x in enumerate(span):
            tall[strided(x), :] = heres[u]
            for c in range(3):
                force[c, x] = ones[c][u]
                field[1, c, x + 2] = news[c][u]
        for c in range(3):
            pack_in(c, news[c], x0)

    forcing(0)
    forcing(bx - 2)
    got_planes = send_planes(1, 1)
    pairs(2, bx - 2, forcing)
    got_packs = send_packs(1)
    jout[...] = tall[...].astype(BF16)
    for p in range(1, PASSES):
        sent = relax(p, got_planes, got_packs)
        if sent is not None:
            got_planes, got_packs = sent
    for src, dst, idx, d in pending:
        @pl.when(exists(d))
        def _(src=src, dst=dst, idx=idx, d=d):
            rdma(src, dst, idx, d).wait_send()


def per_device(
    patches, patch_wx, patch_wy, offset_x, offset_y, block_counts, template, stiff_mu, stiff_lam, start_field
):
    slots, depth, bx, by = patches.shape
    vmem = pl.BlockSpec(memory_space=pltpu.VMEM)
    smem = pl.BlockSpec(memory_space=pltpu.SMEM)
    plane = (depth, by)
    shape = jax.ShapeDtypeStruct
    quads = pl.pallas_call(
        blend_kernel,
        out_shape=(
            shape((bx,) + plane, F32),
            shape((bx, 2) + plane, BF16),
            shape((bx,) + plane, BF16),
            shape((4, bx, by), F32),
        ),
        in_specs=[smem] * 3 + [pl.BlockSpec(memory_space=pltpu.HBM), vmem, vmem],
        out_specs=(vmem,) * 4,
        scratch_shapes=[
            pltpu.VMEM((2, 2 * bx) + plane, F32),
            pltpu.VMEM((2, 2 * bx, 8, by), F32),
            pltpu.VMEM((2, depth * bx, by), F32),
            pltpu.VMEM((slots, depth * bx, by), BF16),
            pltpu.VMEM((slots, bx), F32),
            pltpu.VMEM((slots, by), F32),
            pltpu.SemaphoreType.DMA((slots,)),
        ],
        compiler_params=pltpu.CompilerParams(vmem_limit_bytes=40 * 2**20),
        name="blend",
    )(
        block_counts,
        offset_x.reshape(1, slots),
        offset_y.reshape(1, slots),
        patches.reshape(slots, depth * bx, by),
        patch_wx.reshape(slots, bx),
        patch_wy.reshape(slots, by),
    )
    n_copies = CHUNKS + 1 + 8 + 4 + 1 + CHUNKS + 4 + 8 * (PASSES - 1)
    scratch = [
        ((2, 3, bx + 4) + plane, F32),
        ((bx + 2,) + plane, F32),
        ((bx + 2,) + plane, F32),
        ((8, bx) + plane, F32),
        ((3, bx) + plane, F32),
        ((bx + 2,) + plane, F32),
        ((depth * bx, by), F32),
        ((bx + 2,) + plane, F32),
        ((5,) + plane, F32),
        ((4,) + plane, F32),
        ((2,) + plane, F32),
        ((bx, by), F32),
        ((bx, 2) + plane, BF16),
        ((2, bx, by), F32),
        ((bx,) + plane, BF16),
        ((bx, by), F32),
        ((bx,) + plane, BF16),
        ((bx, by), F32),
        ((PASSES, 2, 3, 2) + plane, BF16),
        ((PASSES, 2, 3, 2) + plane, BF16),
        ((PASSES, 3) + plane, BF16),
        ((PASSES, 2, 3) + plane, BF16),
        ((PASSES, 4, 2) + plane, BF16),
        ((2, 2) + plane, BF16),
        ((2, 2) + plane, BF16),
        ((2,) + plane, BF16),
        ((2, 2) + plane, BF16),
        ((2,) + plane, BF16),
        ((2,) + plane, BF16),
        (plane, BF16),
        ((2,) + plane, BF16),
    ]
    joined, field = pl.pallas_call(
        relax_kernel,
        out_shape=(shape((depth * bx, by), BF16), shape((3, depth * bx, by), F32)),
        in_specs=[vmem] * 8,
        out_specs=(vmem, vmem),
        scratch_shapes=[pltpu.VMEM(dims, kind) for dims, kind in scratch]
        + [pltpu.SemaphoreType.DMA((n_copies,)), pltpu.SemaphoreType.DMA((n_copies,))],
        compiler_params=pltpu.CompilerParams(
            collective_id=0, has_side_effects=True, vmem_limit_bytes=50 * 2**20
        ),
        name="relax",
    )(
        *quads,
        template.reshape(depth * bx, by),
        stiff_mu.reshape(depth * bx, by),
        stiff_lam.reshape(depth * bx, by),
        start_field.reshape(3, depth * bx, by),
    )
    return joined.reshape(depth, bx, by), field.reshape(3, depth, bx, by)


def solution(mesh):
    placed = (
        P(None, None, "gx", "gy"),
        P(None, "gy", "gx"),
        P(None, "gx", "gy"),
        P(None, "gx", "gy"),
        P(None, "gx", "gy"),
        P("gx", "gy"),
        P(None, "gx", "gy"),
        P(None, "gx", "gy"),
        P(None, "gx", "gy"),
        P(None, None, "gx", "gy"),
    )
    return jax.shard_map(
        per_device,
        mesh=mesh,
        in_specs=placed,
        out_specs=(P(None, "gx", "gy"), P(None, None, "gx", "gy")),
        check_vma=False,
    )
```

```python
import functools

import jax
import jax.numpy as jnp
from jax import lax
from jax.experimental import pallas as pl
from jax.experimental.pallas import tpu as pltpu
from jax.sharding import PartitionSpec as P

PASSES = 4
RELAX_FACTOR = 0.9
F32 = jnp.float32
BF16 = jnp.bfloat16
MESH = pl.DeviceIdType.MESH
DIRS = ((1, 0), (-1, 0), (0, 1), (0, -1), (1, 1), (1, -1), (-1, 1), (-1, -1))
CHUNKS = 4
GROUP = 8


def blend_kernel(count, ox_ref, oy_ref, patches, wx_ref, wy_ref, q00, qx, q01, wout, canvas, wcan, res, held, wxf, wyf, arrived):
    by = held.shape[-1]
    bx, depth = q00.shape[:2]
    live = count[0, 0]

    def fetch(s):
        return pltpu.make_async_copy(patches.at[s], held.at[s], arrived.at[s])

    def begin(s, carry):
        fetch(s).start()
        return carry

    lax.fori_loop(0, live, begin, 0)
    canvas[...] = jnp.zeros_like(canvas)
    wcan[...] = jnp.zeros_like(wcan)
    wxf[...] = wx_ref[...].astype(F32)
    wyf[...] = wy_ref[...].astype(F32)
    source = lax.broadcasted_iota(jnp.int32, (by, 2 * by), 0)
    target = lax.broadcasted_iota(jnp.int32, (by, 2 * by), 1)

    def add_patch(s, carry):
        ox = ox_ref[0, s]
        place = jnp.where(target == source + oy_ref[0, s], 1.0, 0.0).astype(BF16)
        fetch(s).wait()
        moved = jnp.dot(held[s], place, preferred_element_type=F32)
        res[0] = moved[:, :by]
        res[1] = moved[:, by:]
        along_y = jnp.broadcast_to(wyf[pl.ds(s, 1), :], (16, by)).astype(BF16)
        wy_row = jnp.dot(along_y, place, preferred_element_type=F32)[:8]
        along_x = jnp.broadcast_to(wxf[pl.ds(s, 1), :], (8, bx))
        for x0 in range(0, bx, 4):
            for h in range(2):
                span = range(x0, x0 + 4)
                weights = [along_x[:, x : x + 1] * wy_row[:, h * by : (h + 1) * by] for x in span]
                sums = [
                    canvas[h, ox + x] + res[h, pl.ds(x, depth, stride=bx), :] * weight[0:1]
                    for x, weight in zip(span, weights)
                ]
                totals = [wcan[h, ox + x] + weight for x, weight in zip(span, weights)]
                for n, x in enumerate(span):
                    canvas[h, ox + x] = sums[n]
                    wcan[h, ox + x] = totals[n]
        return carry

    lax.fori_loop(0, live, add_patch, 0)
    q00[...] = canvas[0, :bx]
    qx[:, 0] = canvas[0, bx:].astype(BF16)
    qx[:, 1] = canvas[1, bx:].astype(BF16)
    q01[...] = canvas[1, :bx].astype(BF16)
    for x in range(bx):
        wout[0, x : x + 1] = wcan[0, x, 0:1]
        wout[1, x : x + 1] = wcan[0, bx + x, 0:1]
        wout[2, x : x + 1] = wcan[1, bx + x, 0:1]
        wout[3, x : x + 1] = wcan[1, x, 0:1]


def relax_kernel(
    q00, qx, q01, wq, tmpl, mu_ref, lam_ref, fld, jout, fout,
    field, mu, qb, coef, force, joined, tall, grad, acc, packed, cpack, wsum,
    land_q, land_w, sy, sw, land_y, land_wy,
    xs, xl, ap, al, dl, cxs, cxl, cap, cal, jxs, jxl, jap, jal,
    send_sem, recv_sem,
):
    bx, depth, by = q00.shape
    gx, gy = lax.axis_index("gx"), lax.axis_index("gy")
    nx, ny = lax.axis_size("gx"), lax.axis_size("gy")

    def exists(d):
        ok = True
        for where, step, count in ((gx, d[0], nx), (gy, d[1], ny)):
            if step == 1:
                ok = jnp.logical_and(ok, where < count - 1)
            if step == -1:
                ok = jnp.logical_and(ok, where > 0)
        return ok

    def opposite(d):
        return (-d[0], -d[1])

    pending = []

    def rdma(src, dst, idx, d):
        return pltpu.make_async_remote_copy(
            src_ref=src, dst_ref=dst, send_sem=send_sem.at[idx], recv_sem=recv_sem.at[idx],
            device_id=(gx + d[0], gy + d[1]), device_id_type=MESH,
        )

    counter = [0]

    def send(src, dst, d):
        idx = counter[0]
        counter[0] += 1

        @pl.when(exists(d))
        def _():
            rdma(src, dst, idx, d).start()

        pending.append((src, dst, idx, d))

        def arrive():
            @pl.when(exists(opposite(d)))
            def _():
                rdma(src, dst, idx, d).wait_recv()

        return arrive

    lane = lax.broadcasted_iota(jnp.int32, (depth, by), 1)
    level = lax.broadcasted_iota(jnp.int32, (depth, by), 0)
    pos = lax.rem(lane, GROUP)

    def strided(x):
        return pl.ds(x, depth, stride=bx)

    def z_next(v):
        return jnp.where(level == depth - 1, 0.0, pltpu.roll(v, depth - 1, 0))

    def z_prev(v):
        return jnp.where(level == 0, 0.0, pltpu.roll(v, 1, 0))

    def y_next(v, edge):
        return jnp.where(lane == by - 1, edge, pltpu.roll(v, by - 1, 1))

    def y_prev(v, edge):
        return jnp.where(lane == 0, edge, pltpu.roll(v, 1, 1))

    def at_edge(pack, x):
        return pltpu.roll(pack, by - 4 - GROUP * x, 1)

    def pack_in(slot, planes, x0):
        out = acc[slot]
        for u, plane in enumerate(planes):
            at = GROUP * (x0 + u)
            own = jnp.logical_and(lane >= at, lane < at + 4)
            out = jnp.where(own, pltpu.roll(plane, (at + 2) % by, 1), out)
        acc[slot] = out

    def pairs(low, high, body):
        def two(n, carry):
            body(2 * n)
            return carry

        lax.fori_loop(low // 2, high // 2, two, 0)

    def merge(own, left, right):
        left, right = left.astype(F32), right.astype(F32)
        out = jnp.where(pos >= 6, pltpu.roll(own, 4, 1), own)
        out = jnp.where(pos == 2, pltpu.roll(left, 2, 1), out)
        out = jnp.where(pos == 4, pltpu.roll(left, 3, 1), out)
        out = jnp.where(pos == 3, pltpu.roll(right, 1, 1), out)
        return jnp.where(pos == 5, pltpu.roll(right, 2, 1), out)

    barrier = pltpu.get_barrier_semaphore()
    total = 0
    for d in DIRS:
        @pl.when(exists(d))
        def _(d=d):
            pl.semaphore_signal(barrier, inc=1, device_id=(gx + d[0], gy + d[1]), device_id_type=MESH)

        total = total + jnp.where(exists(d), 1, 0)

    for k, d in enumerate(DIRS):
        @pl.when(jnp.logical_not(exists(opposite(d))))
        def _(k=k):
            if k == 0:
                land_q[...] = jnp.zeros_like(land_q)
                land_w[...] = jnp.zeros_like(land_w)
            if k == 2:
                land_y[...] = jnp.zeros_like(land_y)
                land_wy[...] = jnp.zeros_like(land_wy)
            if k < 2:
                for p in range(PASSES):
                    xl[p, k] = jnp.zeros(xl.shape[2:], BF16)
                cxl[k] = jnp.zeros(cxl.shape[1:], BF16)
                jxl[k] = jnp.zeros(jxl.shape[1:], BF16)
            elif k < 4:
                for p in range(PASSES):
                    al[p, k - 2] = jnp.zeros(al.shape[2:], BF16)
                cal[k - 2] = jnp.zeros(cal.shape[1:], BF16)
                jal[k - 2] = jnp.zeros(jal.shape[1:], BF16)
            else:
                for p in range(PASSES):
                    dl[p, k - 4] = jnp.zeros(dl.shape[2:], BF16)

    acc[...] = jnp.zeros_like(acc)
    pl.semaphore_wait(barrier, total)

    step = bx // CHUNKS
    got_q = []
    for c in range(CHUNKS):
        part = pl.ds(c * step, step)
        got_q.append(send(qx.at[part], land_q.at[part], (1, 0)))
    got_w = send(wq.at[pl.ds(1, 2)], land_w, (1, 0))

    def load(x0):
        span = (x0, x0 + 1)
        planes = [[fld[c, strided(x), :] for x in span] for c in range(3)]
        mus = [mu_ref[strided(x), :] for x in span]
        bulks = [0.25 * (lam_ref[strided(x), :] + one) for x, one in zip(span, mus)]
        for u, x in enumerate(span):
            for c in range(3):
                field[0, c, x + 2] = planes[c][u]
            mu[x + 1] = mus[u]
            qb[x + 1] = bulks[u]
        for slot, values in enumerate(planes + [mus, bulks]):
            pack_in(slot, values, x0)

    pairs(0, bx, load)

    def send_planes(p, b):
        for c in range(3):
            xs[p, 0, c] = field[b, c, bx : bx + 2].astype(BF16)
            xs[p, 1, c] = field[b, c, 2:4].astype(BF16)
        return [send(xs.at[p, k], xl.at[p, k], DIRS[k]) for k in range(2)]

    def send_packs(p):
        for c in range(3):
            ap[p, c] = acc[c].astype(BF16)
        far = [send(ap.at[p, pl.ds(1, 2)], dl.at[p, k - 4], DIRS[k]) for k in range(4, 8)]
        near = [send(ap.at[p], al.at[p, k - 2], DIRS[k]) for k in range(2, 4)]
        return near, far

    got_planes = send_planes(0, 0)
    got_packs = send_packs(0)
    for k, at in ((0, bx), (1, 1)):
        cxs[k, 0] = mu[at].astype(BF16)
        cxs[k, 1] = qb[at].astype(BF16)
    cap[...] = acc[3:5].astype(BF16)
    got_coef = [send(cxs.at[k], cxl.at[k], DIRS[k]) for k in range(2)]
    got_coef += [send(cap, cal.at[k - 2], DIRS[k]) for k in range(2, 4)]

    got_w()
    sw[...] = wq[3] + land_w[1]
    got_wy = send(sw, land_wy, (0, 1))
    got_y = []

    def pass_on(c):
        part = pl.ds(c * step, step)
        got_q[c]()
        sy[part] = (q01[part].astype(F32) + land_q[part, 1].astype(F32)).astype(BF16)
        got_y.append(send(sy.at[part], land_y.at[part], (0, 1)))

    for c in range(CHUNKS // 2):
        pass_on(c)

    for arrive in got_coef:
        arrive()
    for k, at in ((0, 0), (1, bx + 1)):
        mu[at] = cxl[k, 0].astype(F32)
        qb[at] = cxl[k, 1].astype(F32)
    for c in range(2):
        cpack[c] = merge(acc[3 + c], cal[0, c], cal[1, c])

    def coefficients(x0):
        found = []
        for x in (x0, x0 + 1):
            here = mu[x + 1]
            rate = RELAX_FACTOR / (6.0 * here + 12.0 * qb[x + 1])
            half = 0.5 * rate
            edge = at_edge(cpack[0], x)
            near = (
                z_next(here), z_prev(here), mu[x + 2], mu[x], y_next(here, edge), y_prev(here, edge),
            )
            values = [half * (here + other) for other in near]
            rest = 1.0
            for one in values:
                rest = rest - one
            found.append(values + [rest, rate])
        for u in range(2):
            for n in range(8):
                coef[n, x0 + u] = found[u][n]

    pairs(0, bx, coefficients)
    for c in range(CHUNKS // 2, CHUNKS):
        pass_on(c)

    def relax(p, got_planes, got_packs):
        b, nb = p % 2, 1 - p % 2
        last = p == PASSES - 1
        for arrive in got_packs[0]:
            arrive()
        for c in range(3):
            packed[c] = merge(acc[c], al[p, 0, c], al[p, 1, c])

        def gradient(at, edge):
            vz, vy = field[b, 0, at + 1], field[b, 2, at + 1]
            return qb[at] * (
                (field[b, 1, at + 2] - field[b, 1, at])
                + (z_next(vz) - z_prev(vz))
                + (y_next(vy, edge) - y_prev(vy, edge))
            )

        def inner(span):
            pack = packed[2]
            values = [gradient(x + 1, at_edge(pack, x)) for x in span]
            for x, value in zip(span, values):
                grad[x + 1] = value

        def four(n, carry):
            inner([2 + 4 * n + u for u in range(4)])
            return carry

        lax.fori_loop(0, (bx - 4) // 4, four, 0)
        for arrive in got_planes:
            arrive()
        for c in range(3):
            field[b, c, 0:2] = xl[p, 0, c].astype(F32)
            field[b, c, bx + 2 : bx + 4] = xl[p, 1, c].astype(F32)
        inner([0, 1, bx - 2, bx - 1])
        for arrive in got_packs[1]:
            arrive()
        corner = [[dl[p, k, c].astype(F32) for c in range(2)] for k in range(4)]
        top = GROUP * (bx - 1)

        def bring(k, c, at):
            plus_x, plus_y = DIRS[4 + k]
            source = (top if plus_x == 1 else 0) + (1 if plus_y == 1 else 2)
            return pltpu.roll(corner[k][c], (at - source) % by, 1)

        def edge_corners(low, high):
            return jnp.where(lane == 0, bring(low, 1, 0), bring(high, 1, by - 1))

        vx = packed[1]
        ahead = pltpu.roll(vx, by - GROUP, 1)
        ahead = jnp.where(lane == top + 3, bring(3, 0, top + 3), ahead)
        ahead = jnp.where(lane == top + 4, bring(2, 0, top + 4), ahead)
        behind = pltpu.roll(vx, GROUP, 1)
        behind = jnp.where(lane == 3, bring(1, 0, 3), behind)
        behind = jnp.where(lane == 4, bring(0, 0, 4), behind)
        if GROUP * bx < by:
            ahead = jnp.where(lane >= GROUP * bx, 0.0, ahead)
        vz, vy = packed[0], packed[2]
        packed[3] = cpack[1] * (
            (ahead - behind) + (z_next(vz) - z_prev(vz))
            + (pltpu.roll(vy, by - 2, 1) - pltpu.roll(vy, 2, 1))
        )

        low = gradient(0, edge_corners(0, 1))
        high = gradient(bx + 1, edge_corners(2, 3))
        grad[0] = low
        grad[bx + 1] = high
        if not last:
            acc[0:3] = jnp.zeros((3, depth, by), F32)

        def update(x0):
            news = [[], [], []]
            for x in (x0, x0 + 1):
                g = grad[x + 1]
                g_edge = at_edge(packed[3], x)
                rise = (
                    z_next(g) - z_prev(g),
                    grad[x + 2] - grad[x],
                    y_next(g, g_edge) - y_prev(g, g_edge),
                )
                k = [coef[n, x] for n in range(8)]
                for c in range(3):
                    v = field[b, c, x + 2]
                    edge = at_edge(packed[c], x)
                    new = k[6] * v + k[7] * rise[c]
                    new = new + k[0] * z_next(v) + k[1] * z_prev(v)
                    new = new + k[2] * field[b, c, x + 3] + k[3] * field[b, c, x + 1]
                    new = new + k[4] * y_next(v, edge) + k[5] * y_prev(v, edge)
                    if p > 0:
                        new = new + force[c, x]
                    news[c].append(new)
            for c in range(3):
                for u in range(2):
                    if last:
                        fout[c, strided(x0 + u), :] = news[c][u]
                    else:
                        field[nb, c, x0 + u + 2] = news[c][u]
                if p > 0 and not last:
                    pack_in(c, news[c], x0)

        if p == 0 or last:
            pairs(0, bx, update)
            return None
        update(0)
        update(bx - 2)
        got_planes = send_planes(p + 1, nb)
        pairs(2, bx - 2, update)
        return got_planes, send_packs(p + 1)

    relax(0, got_planes, got_packs)

    got_wy()
    wsum[...] = jnp.maximum(wq[0] + land_w[0] + land_wy[...], 1.0)
    acc[3] = jnp.zeros((depth, by), F32)
    tall[...] = tmpl[...].astype(F32)

    def join(x0):
        planes = []
        for x in (x0, x0 + 1):
            value = q00[x] + land_q[x, 0].astype(F32) + land_y[x].astype(F32)
            planes.append((value / wsum[pl.ds(x, 1), :]).astype(BF16).astype(F32))
        for u in range(2):
            joined[x0 + u + 1] = planes[u]
        pack_in(3, planes, x0)

    for c in range(CHUNKS):
        got_y[c]()
        pairs(c * step, (c + 1) * step, join)
    jxs[0] = joined[bx].astype(BF16)
    jxs[1] = joined[1].astype(BF16)
    jap[...] = acc[3].astype(BF16)
    got = [send(jxs.at[k], jxl.at[k], DIRS[k]) for k in range(2)]
    got += [send(jap, jal.at[k - 2], DIRS[k]) for k in range(2, 4)]
    for arrive in got:
        arrive()
    joined[0] = jxl[0].astype(F32)
    joined[bx + 1] = jxl[1].astype(F32)
    cpack[0] = merge(acc[3], jal[0], jal[1])

    def forcing(x0):
        span = (x0, x0 + 1)
        ones, news, heres = [[], [], []], [[], [], []], []
        for x in span:
            here = joined[x + 1]
            edge = at_edge(cpack[0], x)
            mismatch = (tall[strided(x), :] - here) * 0.5 * coef[7, x]
            slopes = (
                z_next(here) - z_prev(here),
                joined[x + 2] - joined[x],
                y_next(here, edge) - y_prev(here, edge),
            )
            heres.append(here)
            for c in range(3):
                ones[c].append(mismatch * slopes[c])
                news[c].append(field[1, c, x + 2] + ones[c][-1])
        for u, x in enumerate(span):
            tall[strided(x), :] = heres[u]
            for c in range(3):
                force[c, x] = ones[c][u]
                field[1, c, x + 2] = news[c][u]
        for c in range(3):
            pack_in(c, news[c], x0)

    forcing(0)
    forcing(bx - 2)
    got_planes = send_planes(1, 1)
    pairs(2, bx - 2, forcing)
    got_packs = send_packs(1)
    jout[...] = tall[...].astype(BF16)
    for p in range(1, PASSES):
        sent = relax(p, got_planes, got_packs)
        if sent is not None:
            got_planes, got_packs = sent
    for src, dst, idx, d in pending:
        @pl.when(exists(d))
        def _(src=src, dst=dst, idx=idx, d=d):
            rdma(src, dst, idx, d).wait_send()


def per_device(
    patches, patch_wx, patch_wy, offset_x, offset_y, block_counts, template, stiff_mu, stiff_lam, start_field
):
    slots, depth, bx, by = patches.shape
    vmem = pl.BlockSpec(memory_space=pltpu.VMEM)
    smem = pl.BlockSpec(memory_space=pltpu.SMEM)
    plane = (depth, by)
    shape = jax.ShapeDtypeStruct
    quads = pl.pallas_call(
        blend_kernel,
        out_shape=(
            shape((bx,) + plane, F32),
            shape((bx, 2) + plane, BF16),
            shape((bx,) + plane, BF16),
            shape((4, bx, by), F32),
        ),
        in_specs=[smem] * 3 + [pl.BlockSpec(memory_space=pltpu.HBM), vmem, vmem],
        out_specs=(vmem,) * 4,
        scratch_shapes=[
            pltpu.VMEM((2, 2 * bx) + plane, F32),
            pltpu.VMEM((2, 2 * bx, 8, by), F32),
            pltpu.VMEM((2, depth * bx, by), F32),
            pltpu.VMEM((slots, depth * bx, by), BF16),
            pltpu.VMEM((slots, bx), F32),
            pltpu.VMEM((slots, by), F32),
            pltpu.SemaphoreType.DMA((slots,)),
        ],
        compiler_params=pltpu.CompilerParams(vmem_limit_bytes=62 * 2**20),
        name="blend",
    )(
        block_counts,
        offset_x.reshape(1, slots),
        offset_y.reshape(1, slots),
        patches.reshape(slots, depth * bx, by),
        patch_wx.reshape(slots, bx),
        patch_wy.reshape(slots, by),
    )
    n_copies = CHUNKS + 1 + 8 + 4 + 1 + CHUNKS + 4 + 8 * (PASSES - 1)
    scratch = [
        ((2, 3, bx + 4) + plane, F32),
        ((bx + 2,) + plane, F32),
        ((bx + 2,) + plane, F32),
        ((8, bx) + plane, F32),
        ((3, bx) + plane, F32),
        ((bx + 2,) + plane, F32),
        ((depth * bx, by), F32),
        ((bx + 2,) + plane, F32),
        ((5,) + plane, F32),
        ((4,) + plane, F32),
        ((2,) + plane, F32),
        ((bx, by), F32),
        ((bx, 2) + plane, BF16),
        ((2, bx, by), F32),
        ((bx,) + plane, BF16),
        ((bx, by), F32),
        ((bx,) + plane, BF16),
        ((bx, by), F32),
        ((PASSES, 2, 3, 2) + plane, BF16),
        ((PASSES, 2, 3, 2) + plane, BF16),
        ((PASSES, 3) + plane, BF16),
        ((PASSES, 2, 3) + plane, BF16),
        ((PASSES, 4, 2) + plane, BF16),
        ((2, 2) + plane, BF16),
        ((2, 2) + plane, BF16),
        ((2,) + plane, BF16),
        ((2, 2) + plane, BF16),
        ((2,) + plane, BF16),
        ((2,) + plane, BF16),
        (plane, BF16),
        ((2,) + plane, BF16),
    ]
    joined, field = pl.pallas_call(
        relax_kernel,
        out_shape=(shape((depth * bx, by), BF16), shape((3, depth * bx, by), F32)),
        in_specs=[vmem] * 8,
        out_specs=(vmem, vmem),
        scratch_shapes=[pltpu.VMEM(dims, kind) for dims, kind in scratch]
        + [pltpu.SemaphoreType.DMA((n_copies,)), pltpu.SemaphoreType.DMA((n_copies,))],
        compiler_params=pltpu.CompilerParams(
            collective_id=0, has_side_effects=True, vmem_limit_bytes=62 * 2**20
        ),
        name="relax",
    )(
        *quads,
        template.reshape(depth * bx, by),
        stiff_mu.reshape(depth * bx, by),
        stiff_lam.reshape(depth * bx, by),
        start_field.reshape(3, depth * bx, by),
    )
    return joined.reshape(depth, bx, by), field.reshape(3, depth, bx, by)


def solution(mesh):
    placed = (
        P(None, None, "gx", "gy"),
        P(None, "gy", "gx"),
        P(None, "gx", "gy"),
        P(None, "gx", "gy"),
        P(None, "gx", "gy"),
        P("gx", "gy"),
        P(None, "gx", "gy"),
        P(None, "gx", "gy"),
        P(None, "gx", "gy"),
        P(None, None, "gx", "gy"),
    )
    return jax.shard_map(
        per_device,
        mesh=mesh,
        in_specs=placed,
        out_specs=(P(None, "gx", "gy"), P(None, None, "gx", "gy")),
        check_vma=False,
    )
```
